32 devices in a mesh: tm: 4 (over z), tile: 8 (over y, x, core).
Axes of the slice: x: 2, y: 2, z: 4, core: 2. Of those that a mesh axis runs over, the one named last changes fastest.
Arguments:
- heads: float32 [4, 3, 128, 4096], P('tm', None, 'tile'), may hold values from -6 to 6
- capacity: float32 [128, 4096], P('tile'), may hold values from 0.5 to 2
- cond_row: float32 [128, 4096], P('tile'), may hold values from 0.1 to 1
- cond_col: float32 [128, 4096], P('tile'), may hold values from 0.1 to 1
- terminal: float32 [2, 128, 4096], P(None, 'tile'), may hold values from -6 to 6
- obs_cell: int32 [4, 2, 512], P('tm'), may hold values from 0 to 524287
- obs_weight: float32 [4, 2, 2, 512], P('tm'), may hold values from -8 to 8
- block_mask: int32 [1, 32], replicated, may hold values 0 or 1
Outputs:
- adjoint_start: float32 [4, 2, 128, 4096], P('tm', None, 'tile')
- cond_sens: float32 [128, 4096], P('tile', 'tm')
- storage_sens: float32 [2], replicated
The draws below stay inside these ranges and needn't reach their ends.
Inputs may be any that keep to these rules, and one draw needn't show every extreme that they name: `obs_cell`: row * 4096 + column of an observed cell; a cell may repeat.
All inputs are finite; a program needn't handle non-finite values.
Results may differ from the reference program's by a relative error of at most 0.0003.
Values sent between devices are 32-bit elements; how exact they have to be, the bound alone decides.
No kernel may reach another device: no remote copies, remote signals or barrier semaphores. Data moves between devices by JAX's collectives and lax.ppermute only.
A program may use at most 64 MiB of HBM per device.

```python
import math
import jax
import jax.numpy as jnp

NY = 4096
BLOCK = 128
MEMBERS = 2
NOBS = 512
STEPS = 2
SWEEPS = 2
SECTIONS = 4
NX = 128


def with_ends(values, rng, least, top_value):
    spot = [jax.random.randint(jax.random.fold_in(rng, axis), (), 0, length) for axis, length in enumerate(values.shape)]
    widest = values.shape.index(max(values.shape))
    neighbour = spot[:widest] + [(spot[widest] + 1) % values.shape[widest]] + spot[widest + 1:]
    return values.at[tuple(spot)].set(least).at[tuple(neighbour)].set(top_value)


def steps_of(own_key, extent, cuts, least, high):
    def one(dim, shards_of):
        steps = jax.random.uniform(jax.random.fold_in(jax.random.fold_in(own_key, 6), dim), (shards_of,), jnp.float32, least / len(cuts), high / len(cuts))
        return jnp.repeat(jnp.exp(steps), extent[dim] // shards_of).reshape((-1,) + (1,) * (len(extent) - dim - 1))

    gain = one(*cuts[0])
    for cut in cuts[1:]:
        gain = gain * one(*cut)
    return gain


def bell_draw(rng, dims, width, limit, pieces=(), kind=jnp.bfloat16):
    result = width * jax.random.normal(rng, dims, jnp.float32)
    if pieces:
        result = result * steps_of(rng, dims, pieces, -0.22, 0.18)
    return jnp.clip(result, -limit, limit).astype(kind)


def setup_inputs(seed: int = 0) -> dict:
    streams_of = jax.random.split(jax.random.key(seed), 9)
    heads = bell_draw(streams_of[0], (SECTIONS, STEPS + 1, NX, NY), 1.0, 6.0, ((0, 4), (2, 8)), jnp.float32)
    capacity = jnp.clip(jnp.exp(math.log(2.0) - 1.3862944 * jax.random.uniform(streams_of[1], (NX, NY), jnp.float32) ** steps_of(streams_of[1], (NX, NY), ((0, 8),), -0.2, 0.2)), 0.5, 2.0)
    cond_row = jnp.clip(jnp.exp(math.log(1.0) - 2.3025851 * jax.random.uniform(streams_of[2], (NX, NY), jnp.float32) ** steps_of(streams_of[2], (NX, NY), ((0, 8),), -0.2, 0.2)), 0.1, 1.0)
    cond_col = jnp.clip(jnp.exp(math.log(1.0) - 2.3025851 * jax.random.uniform(streams_of[3], (NX, NY), jnp.float32) ** steps_of(streams_of[3], (NX, NY), ((0, 8),), -0.2, 0.2)), 0.1, 1.0)
    terminal = bell_draw(streams_of[4], (MEMBERS, NX, NY), 1.0, 6.0, ((1, 8),), jnp.float32)
    obs_cell = with_ends(jax.random.randint(streams_of[5], (SECTIONS, STEPS, NOBS), 0, NX * NY), jax.random.fold_in(streams_of[5], 1), 0, (NX * NY) - 1).astype(jnp.int32)
    obs_weight = bell_draw(streams_of[6], (SECTIONS, STEPS, MEMBERS, NOBS), 2.0, 8.0, ((0, 4),), jnp.float32)
    block_mask = with_ends((jax.random.randint(streams_of[7], (NX // BLOCK, NY // BLOCK), 0, 4) < 3).astype(jnp.int32), jax.random.fold_in(streams_of[7], 1), 0, 1)
    return {"heads": heads, "capacity": capacity, "cond_row": cond_row, "cond_col": cond_col, "terminal": terminal, "obs_cell": obs_cell, "obs_weight": obs_weight, "block_mask": block_mask}


def relax(field, rhs, east, west, south, north, diagonal):
    padded = jnp.pad(field, ((0, 0), (1, 1), (1, 1)))
    above = padded[:, :-2, 1:-1]
    below = padded[:, 2:, 1:-1]
    left = padded[:, 1:-1, :-2]
    right = padded[:, 1:-1, 2:]
    return (rhs + east * right + west * left + south * below + north * above) / diagonal


def reference(heads, capacity, cond_row, cond_col, terminal, obs_cell, obs_weight, block_mask):
    active = jnp.repeat(jnp.repeat(block_mask.astype(jnp.float32), BLOCK, axis=0), BLOCK, axis=1)
    zero_col = jnp.zeros((NX, 1), jnp.float32)
    zero_row = jnp.zeros((1, NY), jnp.float32)
    pair = active * jnp.concatenate([active[:, 1:], zero_col], axis=1)
    east = cond_row * pair
    west = jnp.concatenate([zero_col, east[:, :-1]], axis=1)
    next_active = jnp.concatenate([active[1:], zero_row], axis=0)
    south = cond_col * active * next_active
    north = jnp.concatenate([zero_row, south[:-1]], axis=0)
    diagonal = capacity + east + west + south + north
    field = terminal
    starts = []
    sens = jnp.zeros((NX, NY), jnp.float32)
    storage = jnp.zeros((MEMBERS,), jnp.float32)
    zero_cols = jnp.zeros((MEMBERS, NX, 1), jnp.float32)
    for section in reversed(range(SECTIONS)):
        for step in reversed(range(STEPS)):
            cells = obs_cell[section, step]
            cell_row = cells // NY
            cell_col = cells % NY
            force = jnp.zeros((MEMBERS, NX, NY), jnp.float32).at[:, cell_row, cell_col].add(obs_weight[section, step])
            rhs = active * (capacity * field + force)
            for sweep_index in range(SWEEPS):
                field = relax(field, rhs, east, west, south, north, diagonal)
            later = heads[section, step + 1]
            earlier = heads[section, step]
            head_step = jnp.concatenate([later[:, 1:] - later[:, :-1], zero_col], axis=1)
            adj_step = jnp.concatenate([field[:, :, 1:] - field[:, :, :-1], zero_cols], axis=2)
            sens = sens + jnp.sum(adj_step * head_step * pair, axis=0)
            storage = storage + jnp.sum(field * capacity * (later - earlier), axis=(1, 2))
        starts.insert(0, field)
    return jnp.stack(starts), sens, storage
```

```python
import functools

import jax
import jax.numpy as jnp
from jax import lax
from jax.experimental import pallas as pl
from jax.experimental.pallas import tpu as pltpu
from jax.sharding import PartitionSpec as P

BLOCK = 128
STEPS = 2
SWEEPS = 2
LANES = 128
WIDE = 256
F32 = jnp.float32
BF16 = jnp.bfloat16
VMEM_LIMIT = 40 * 2**20


def peer(index, hop, count):
    if count & (count - 1) == 0:
        return index ^ hop
    return (index + hop) % count


def fetch(value, axis, hop):
    count = lax.axis_size(axis)
    return lax.ppermute(value, axis, [(peer(i, hop, count), i) for i in range(count)])


def gather(value, axis):
    count = lax.axis_size(axis)
    blocks, hop = (value[None], 1)
    while hop < count:
        blocks = jnp.concatenate([blocks, fetch(blocks[: count - hop], axis, hop)], axis=0)
        hop *= 2
    return blocks


def total(value, axes):
    for axis in axes:
        count = lax.axis_size(axis)
        if count & (count - 1):
            value = lax.psum(value, axis)
            continue
        hop = 1
        while hop < count:
            value = value + fetch(value, axis, hop)
            hop *= 2
    return value


def inner_pairs(value):
    count = lax.axis_size("tile")
    pairs = [(i, i ^ 1) for i in range(count) if i ^ 1 < count]
    return lax.ppermute(value, "tile", pairs)


def outer_pairs(value):
    count = lax.axis_size("tile")
    low = range(1, count - 1, 2)
    return lax.ppermute(value, "tile", [(i, i + 1) for i in low] + [(i + 1, i) for i in low])


class Plan:
    def __init__(self, rows, width, sections, members, observed):
        self.rows, self.width, self.sections = (rows, width, sections)
        self.members, self.observed = (members, observed)
        self.own = width // sections
        sweeps = sections * STEPS * SWEEPS
        halo = -(-sweeps // LANES) * LANES
        wide = -(-(self.own + 2 * halo) // WIDE) * WIDE
        self.window = min(width, wide)
        self.halo = halo
        self.ext = 3 * rows
        self.per_phase = max(1, rows // (STEPS * SWEEPS))
        self.head_window = min(width, self.own + LANES)

    def start(self, index):
        first = index * self.own - self.halo
        return pl.multiple_of(jnp.clip(first, 0, self.width - self.window), LANES)

    def head_start(self, index):
        return pl.multiple_of(jnp.minimum(index * self.own, self.width - self.head_window), LANES)


def pack_kernel(plan, heads, capacity, cond_row, cond_col, terminal, packed, *rest):
    head_outs, sems = (rest[:-1], rest[-1])
    me = lax.axis_index("tm")
    columns = pl.ds(plan.start(me), plan.window)
    copies = [
        (capacity.at[:, columns], packed.at[0]),
        (cond_row.at[:, columns], packed.at[1]),
        (cond_col.at[:, columns], packed.at[2]),
        (terminal.at[:, :, columns], packed.at[pl.ds(3, plan.members)]),
    ]
    for hop, out in enumerate(head_outs, 1):
        target = peer(me, hop, plan.sections)
        if plan.sections & (plan.sections - 1):
            target = (me - hop + plan.sections) % plan.sections
        copies.append((heads.at[0, :, :, pl.ds(plan.head_start(target), plan.head_window)], out))
    started = [pltpu.make_async_copy(a, b, sems.at[i]) for i, (a, b) in enumerate(copies)]
    for copy in started:
        copy.start()
    for copy in started:
        copy.wait()


def chain_kernel(plan, top, count, mask, packed, inner, outer, *rest):
    first = top == plan.sections - 1
    if first:
        obs, rest = (rest[0], rest[1:])
        field = None
    else:
        field, field_inner, field_outer, obs = rest[:4]
        rest = rest[4:]
    history_out = rest[0]
    last = top - count + 1 == 0
    single = first and last
    send_outs = rest[1 : 1 + plan.sections] if single else ()
    rest = rest[1 + len(send_outs) :]
    grid, east, west, south, north, act_rd, cap_rd, x0, x1, force, history, sems = rest
    me = lax.axis_index("tm")
    tile = lax.axis_index("tile")
    rows, ext, members = (plan.rows, plan.ext, plan.members)
    tiles = plan.window // LANES
    start = plan.start(me)
    inner_at = pl.multiple_of(jnp.where(tile % 2 == 0, 2 * rows, 0), rows)
    outer_at = pl.multiple_of(2 * rows - inner_at, rows)
    places = [(packed, rows), (inner, inner_at), (outer, outer_at)]
    copies = [(ref, grid.at[:, pl.ds(at, rows), :]) for ref, at in places]
    if not first:
        places = [(field, rows), (field_inner, inner_at), (field_outer, outer_at)]
        copies += [(ref, x0.at[:, pl.ds(at, rows), :]) for ref, at in places]
    started = [pltpu.make_async_copy(a, b, sems.at[i]) for i, (a, b) in enumerate(copies)]
    for copy in started:
        copy.start()
    for copy in started:
        copy.wait()

    lane = lax.broadcasted_iota(jnp.int32, (1, LANES), 1)
    ends = lane == LANES - 1
    begins = lane == 0
    tile_rows = lax.axis_size("tile") * rows

    def chunk_active(chunk, column):
        if column >= tiles:
            return jnp.float32(0.0)
        row = (tile + chunk - 1) * rows
        inside = (row >= 0) & (row < tile_rows)
        block = jnp.clip(row, 0, tile_rows - 1) // BLOCK
        value = mask[block, (start + column * LANES) // BLOCK]
        return jnp.where(inside, value, 0).astype(F32)

    def active(column):
        parts = [jnp.full((rows, LANES), chunk_active(chunk, column), F32) for chunk in range(3)]
        return jnp.concatenate(parts, axis=0)

    def cols(column):
        return pl.ds(column * LANES, LANES)

    row_id = lax.broadcasted_iota(jnp.int32, (ext, LANES), 0)
    act = active(0)
    previous = jnp.zeros((ext, LANES), F32)
    for c in range(tiles):
        act_next = active(c + 1)
        pair = act * jnp.where(ends, act_next, act)
        e = grid[1, :, cols(c)] * pair
        w = pltpu.roll(jnp.where(ends, previous, e), 1, axis=1)
        below = jnp.where(row_id == ext - 1, 0.0, pltpu.roll(act, ext - 1, axis=0))
        s = grid[2, :, cols(c)] * act * below
        n = jnp.where(row_id == 0, 0.0, pltpu.roll(s, 1, axis=0))
        cap = grid[0, :, cols(c)]
        diagonal = cap + e + w + s + n
        inverse = jnp.where(diagonal > 0.0, 1.0 / jnp.where(diagonal > 0.0, diagonal, 1.0), 0.0)
        east[:, cols(c)] = e * inverse
        west[:, cols(c)] = w * inverse
        south[:, cols(c)] = s * inverse
        north[:, cols(c)] = n * inverse
        act_rd[:, cols(c)] = act * inverse
        cap_rd[:, cols(c)] = act * cap * inverse
        if first:
            x0[:, :, cols(c)] = grid[pl.ds(3, members), :, cols(c)]
        previous = e
        act = act_next

    wides = plan.window // WIDE

    def observe(section, step, low, height):
        block = peer(section, me, plan.sections)
        if plan.sections & (plan.sections - 1):
            block = (section - me + plan.sections) % plan.sections
        lines = obs[block]
        row = lines[4 * step : 4 * step + 1] - ((tile - 1) * rows + low).astype(F32)
        col = lines[4 * step + 1 : 4 * step + 2] - start.astype(F32)
        inside = (row >= 0.0) & (row < height) & (col >= 0.0) & (col < plan.window)
        group = jnp.floor(col * (1.0 / WIDE))
        key = jnp.where(inside, group * height + row, -1.0).astype(jnp.int32)
        within = (col - group * WIDE).astype(jnp.int32)
        ids = lax.broadcasted_iota(jnp.int32, (wides * height, plan.observed), 0)
        hit = ids == key
        left = []
        for m in range(members):
            weight = lines[4 * step + 2 + m : 4 * step + 3 + m]
            parts = []
            for _ in range(3):
                piece = weight.astype(BF16).astype(F32)
                parts.append(jnp.where(hit, piece, 0.0).astype(BF16))
                weight = weight - piece
            left.append(jnp.concatenate(parts, axis=1))
        place = lax.broadcasted_iota(jnp.int32, (WIDE, plan.observed), 0)
        right = jnp.where(place == within, 1.0, 0.0).astype(BF16)
        right = jnp.concatenate([right] * 3, axis=1)
        found = lax.dot_general(
            jnp.concatenate(left, axis=0),
            right,
            (((1,), (1,)), ((), ())),
            preferred_element_type=F32,
        )
        for m in range(members):
            for g in range(wides):
                at = (m * wides + g) * height
                force[m, low : low + height, g * WIDE : (g + 1) * WIDE] = found[at : at + height]

    def sweep(source, target, low, height, initial):
        band = slice(low, low + height)
        for m in range(members):
            here = source[m, band, cols(0)]
            turned = pltpu.roll(here, LANES - 1, axis=1)
            left = jnp.zeros((height, LANES), F32)
            for c in range(tiles):
                if c + 1 < tiles:
                    after = source[m, band, cols(c + 1)]
                    after_turned = pltpu.roll(after, LANES - 1, axis=1)
                else:
                    after = after_turned = jnp.zeros((height, LANES), F32)
                back = pltpu.roll(here, 1, axis=1)
                x_east = jnp.where(ends, after_turned, turned)
                x_west = jnp.where(begins, left, back)
                x_south = pltpu.roll(here, height - 1, axis=0)
                x_north = pltpu.roll(here, 1, axis=0)
                if initial:
                    rhs = cap_rd[band, cols(c)] * here + act_rd[band, cols(c)] * force[m, band, cols(c)]
                    force[m, band, cols(c)] = rhs
                else:
                    rhs = force[m, band, cols(c)]
                target[m, band, cols(c)] = (
                    rhs
                    + east[band, cols(c)] * x_east
                    + west[band, cols(c)] * x_west
                    + south[band, cols(c)] * x_south
                    + north[band, cols(c)] * x_north
                )
                left, here, turned = (back, after, after_turned)

    def one_section(low, height, number):
        section = top - number
        for step in reversed(range(STEPS)):
            observe(section, step, low, height)
            refs = (x0, x1)
            for index in range(SWEEPS):
                sweep(refs[index % 2], refs[(index + 1) % 2], low, height, index == 0)
            if SWEEPS % 2:
                x0[:, low : low + height, :] = x1[:, low : low + height, :]
            history[section - (top - count + 1), step] = x0[:, rows : 2 * rows, :]

    done = 0
    while done < count:
        low = done * STEPS * SWEEPS // 8 * 8
        until = done + 1
        while until < count and until * STEPS * SWEEPS // 8 * 8 == low:
            until += 1
        lax.fori_loop(done, until, lambda i, _, low=low: one_section(low, ext - 2 * low, i), None)
        done = until

    copies = [(history, history_out)]
    own = pl.ds(pl.multiple_of(me * plan.own - start, LANES), plan.own)
    for hop, out in enumerate(send_outs):
        copies.append((history.at[target_of(plan, me, hop), 0, :, :, own], out))
    started = [pltpu.make_async_copy(a, b, sems.at[i]) for i, (a, b) in enumerate(copies)]
    for copy in started:
        copy.start()
    for copy in started:
        copy.wait()


def target_of(plan, me, hop):
    if plan.sections & (plan.sections - 1):
        return (me - hop + plan.sections) % plan.sections
    return peer(me, hop, plan.sections)


def split_kernel(plan, history, *rest):
    outs, sems = (rest[:-1], rest[-1])
    me = lax.axis_index("tm")
    own = pl.ds(pl.multiple_of(me * plan.own - plan.start(me), LANES), plan.own)
    started = [
        pltpu.make_async_copy(history.at[target_of(plan, me, hop), 0, :, :, own], out, sems.at[hop])
        for hop, out in enumerate(outs)
    ]
    for copy in started:
        copy.start()
    for copy in started:
        copy.wait()


def join_kernel(plan, *rest):
    blocks, out, sems = (rest[:-2], rest[-2], rest[-1])
    me = lax.axis_index("tm")
    started = []
    for hop, block in enumerate(blocks):
        at = pl.multiple_of(peer(me, hop, plan.sections) * plan.own, LANES)
        started.append(pltpu.make_async_copy(block, out.at[:, :, pl.ds(at, plan.own)], sems.at[hop]))
    for copy in started:
        copy.start()
    for copy in started:
        copy.wait()


def sens_kernel(plan, mask, packed, history_in, heads, *rest):
    received, rest = (rest[: plan.sections - 1], rest[plan.sections - 1 :])
    cond_out, storage_out, cap, adj, head, sems = rest
    me = lax.axis_index("tm")
    tile = lax.axis_index("tile")
    rows, members = (plan.rows, plan.members)
    start, head_start = (plan.start(me), plan.head_start(me))
    copies = [(packed.at[0], cap), (history_in, adj)]
    copies.append((heads.at[0, :, :, pl.ds(head_start, plan.head_window)], head.at[0]))
    for hop, ref in enumerate(received, 1):
        copies.append((ref, head.at[hop]))
    started = [pltpu.make_async_copy(a, b, sems.at[i]) for i, (a, b) in enumerate(copies)]
    for copy in started:
        copy.start()
    for copy in started:
        copy.wait()

    ends = lax.broadcasted_iota(jnp.int32, (1, LANES), 1) == LANES - 1
    tiles = plan.own // LANES

    def after(here, following):
        return jnp.where(ends, pltpu.roll(following, LANES - 1, axis=1), pltpu.roll(here, LANES - 1, axis=1))

    own = me * plan.own - start
    head_own = me * plan.own - head_start
    block_row = tile * rows // BLOCK
    columns = plan.width // LANES
    stored = [jnp.zeros((rows, LANES), F32) for _ in range(members)]
    for t in range(tiles):
        here = pl.ds(pl.multiple_of(own + t * LANES, LANES), LANES)
        there = pl.ds(pl.multiple_of(jnp.minimum(own + (t + 1) * LANES, plan.window - LANES), LANES), LANES)
        head_here = pl.ds(pl.multiple_of(head_own + t * LANES, LANES), LANES)
        head_next = jnp.minimum(head_own + (t + 1) * LANES, plan.head_window - LANES)
        head_there = pl.ds(pl.multiple_of(head_next, LANES), LANES)
        column = me * tiles + t
        act = mask[block_row, column].astype(F32)
        act_next = mask[block_row, jnp.minimum(column + 1, columns - 1)].astype(F32)
        act_next = jnp.where(column + 1 < columns, act_next, 0.0)
        pair = act * jnp.where(ends, act_next, act)
        capacity = cap[:, here]
        sens = jnp.zeros((rows, LANES), F32)
        for hop in range(plan.sections):
            section = peer(me, hop, plan.sections)
            levels = [head[hop, k, :, head_here] for k in range(STEPS + 1)]
            for step in range(STEPS):
                fields = [adj[section, step, m, :, here] for m in range(members)]
                rise = capacity * (levels[step + 1] - levels[step])
                for m in range(members):
                    stored[m] = stored[m] + fields[m] * rise
                both = functools.reduce(jnp.add, fields)
                both_next = functools.reduce(jnp.add, [adj[section, step, m, :, there] for m in range(members)])
                slope = after(levels[step + 1], head[hop, step + 1, :, head_there]) - levels[step + 1]
                sens = sens + (after(both, both_next) - both) * slope
        cond_out[:, t * LANES : (t + 1) * LANES] = sens * pair
    storage_out[...] = jnp.zeros((8, LANES), F32)
    for m in range(members):
        storage_out[m : m + 1, :] = jnp.full((1, LANES), jnp.sum(stored[m]), F32)


def shards(heads, capacity, cond_row, cond_col, terminal, obs_cell, obs_weight, block_mask):
    rows, width = capacity.shape
    members = terminal.shape[0]
    sections = lax.axis_size("tm")
    plan = Plan(rows, width, sections, members, obs_cell.shape[2])
    anywhere = pl.BlockSpec(memory_space=pl.ANY)
    in_vmem = pl.BlockSpec(memory_space=pltpu.VMEM)
    in_smem = pl.BlockSpec(memory_space=pltpu.SMEM)
    params = pltpu.CompilerParams(vmem_limit_bytes=VMEM_LIMIT)

    def shape(*dims):
        return jax.ShapeDtypeStruct(dims, F32)

    window = plan.window
    ext = plan.ext
    packed, *head_sends = pl.pallas_call(
        functools.partial(pack_kernel, plan),
        out_shape=[shape(3 + members, rows, window)]
        + [shape(STEPS + 1, rows, plan.head_window)] * (sections - 1),
        in_specs=[anywhere] * 5,
        out_specs=[in_vmem] * sections,
        scratch_shapes=[pltpu.SemaphoreType.DMA((3 + sections,))],
        name="pack",
    )(heads, capacity, cond_row, cond_col, terminal)
    outer = outer_pairs(packed)
    inner = inner_pairs(packed)

    cells = obs_cell[0]
    lines = []
    for step in range(STEPS):
        lines += [(cells[step] // width).astype(F32), (cells[step] % width).astype(F32)]
        lines += [obs_weight[0, step, m] for m in range(members)]
    obs = gather(jnp.stack(lines), "tm")
    received = [fetch(part, "tm", hop) for hop, part in enumerate(head_sends, 1)]

    block = (members, rows, plan.own)
    histories = []
    top = sections - 1
    field = []
    sends = None
    while top >= 0:
        count = min(plan.per_phase, top + 1)
        single = count == sections
        outs = [shape(count, STEPS, members, rows, window)]
        outs += [shape(*block)] * (sections if single else 0)
        plane = pltpu.VMEM((ext, window), F32)
        fields = pltpu.VMEM((members, ext, window), F32)
        results = pl.pallas_call(
            functools.partial(chain_kernel, plan, top, count),
            out_shape=outs,
            in_specs=[in_smem] + [anywhere] * (3 + len(field)) + [in_vmem],
            out_specs=[anywhere] * len(outs),
            scratch_shapes=[
                pltpu.VMEM((3 + members, ext, window), F32),
                *([plane] * 6),
                *([fields] * 3),
                pltpu.VMEM((count, STEPS, members, rows, window), F32),
                pltpu.SemaphoreType.DMA((max(6, 1 + sections),)),
            ],
            compiler_params=params,
            name="chain",
        )(block_mask, packed, inner, outer, *field, obs)
        histories.insert(0, results[0])
        if single:
            sends = results[1:]
        top -= count
        if top >= 0:
            reached = results[0][0, 0]
            field = [reached, inner_pairs(reached), outer_pairs(reached)]
    history = histories[0] if len(histories) == 1 else jnp.concatenate(histories, axis=0)
    if sends is None:
        sends = pl.pallas_call(
            functools.partial(split_kernel, plan),
            out_shape=[shape(*block)] * sections,
            in_specs=[anywhere],
            out_specs=[in_vmem] * sections,
            scratch_shapes=[pltpu.SemaphoreType.DMA((sections,))],
            name="split",
        )(history)

    cond, storage = pl.pallas_call(
        functools.partial(sens_kernel, plan),
        out_shape=[shape(rows, plan.own), shape(8, LANES)],
        in_specs=[in_smem] + [anywhere] * (2 + sections),
        out_specs=[in_vmem, in_vmem],
        scratch_shapes=[
            pltpu.VMEM((rows, window), F32),
            pltpu.VMEM((sections, STEPS, members, rows, window), F32),
            pltpu.VMEM((sections, STEPS + 1, rows, plan.head_window), F32),
            pltpu.SemaphoreType.DMA((2 + sections,)),
        ],
        compiler_params=params,
        name="sens",
    )(block_mask, packed, history, heads, *received)

    blocks = [sends[0]] + [fetch(part, "tm", hop) for hop, part in enumerate(sends[1:], 1)]
    adjoint = pl.pallas_call(
        functools.partial(join_kernel, plan),
        out_shape=shape(members, rows, width),
        in_specs=[anywhere] * sections,
        out_specs=in_vmem,
        scratch_shapes=[pltpu.SemaphoreType.DMA((sections,))],
        name="join",
    )(*blocks)
    storage = total(storage, ("tile", "tm"))
    return (adjoint[None], cond, storage[:members, 0])


def solution(mesh):
    placed = (
        P("tm", None, "tile", None),
        P("tile", None),
        P("tile", None),
        P("tile", None),
        P(None, "tile", None),
        P("tm", None, None),
        P("tm", None, None, None),
        P(),
    )
    return jax.shard_map(
        shards,
        mesh=mesh,
        in_specs=placed,
        out_specs=(P("tm", None, "tile", None), P("tile", "tm"), P()),
        check_vma=False,
    )
```

```python
import functools

import jax
import jax.numpy as jnp
from jax import lax
from jax.experimental import pallas as pl
from jax.experimental.pallas import tpu as pltpu
from jax.sharding import PartitionSpec as P

BLOCK = 128
STEPS = 2
SWEEPS = 2
LANES = 128
WIDE = 256
PIECES = 3
F32 = jnp.float32
BF16 = jnp.bfloat16
VMEM_LIMIT = 24 * 2**20


def fetch(value, axis, hop):
    count = lax.axis_size(axis)
    return lax.ppermute(value, axis, [(i ^ hop, i) for i in range(count)])


def gather(value, axis):
    blocks, hop = (value[None], 1)
    while hop < lax.axis_size(axis):
        blocks = jnp.concatenate([blocks, fetch(blocks, axis, hop)], axis=0)
        hop *= 2
    return blocks


def total(value, axis, hop=1, until=None):
    while hop < (until or lax.axis_size(axis)):
        value = value + fetch(value, axis, hop)
        hop *= 2
    return value


def inner_pairs(value):
    count = lax.axis_size("tile")
    pairs = [(i, i ^ 1) for i in range(count) if i ^ 1 < count]
    return lax.ppermute(value, "tile", pairs)


def outer_pairs(value):
    count = lax.axis_size("tile")
    low = range(1, count - 1, 2)
    return lax.ppermute(value, "tile", [(i, i + 1) for i in low] + [(i + 1, i) for i in low])


class Plan:
    def __init__(self, rows, width, sections, members, observed):
        self.rows, self.width, self.sections = (rows, width, sections)
        self.members, self.observed = (members, observed)
        self.half = width // 2
        sweeps = sections * STEPS * SWEEPS
        self.halo = -(-sweeps // LANES) * LANES
        self.window = self.half + self.halo
        self.tiles = self.window // LANES
        self.ext = 3 * rows
        self.per_phase = max(1, rows // (STEPS * SWEEPS))
        self.groups = sections // 2
        self.out_columns = width // sections

    def start(self, index):
        return pl.multiple_of((index % 2) * (self.half - self.halo), LANES)

    def own(self, index):
        return pl.multiple_of((index % 2) * self.halo, LANES)

    def bands(self, top, count):
        done = 0
        while done < count:
            low = done * STEPS * SWEEPS // 8 * 8
            until = done + 1
            while until < count and until * STEPS * SWEEPS // 8 * 8 == low:
                until += 1
            yield done, until, low
            done = until


def run_copies(copies, sems):
    started = [pltpu.make_async_copy(a, b, sems.at[i]) for i, (a, b) in enumerate(copies)]
    for copy in started:
        copy.start()
    for copy in started:
        copy.wait()


def pack_kernel(plan, capacity, cond_row, cond_col, terminal, packed, sems):
    columns = pl.ds(plan.start(lax.axis_index("tm")), plan.window)
    copies = [
        (capacity.at[:, columns], packed.at[0]),
        (cond_row.at[:, columns], packed.at[1]),
        (cond_col.at[:, columns], packed.at[2]),
        (terminal.at[:, :, columns], packed.at[pl.ds(3, plan.members)]),
    ]
    run_copies(copies, sems)


def heads_kernel(plan, heads, out, sems):
    others = pl.ds(plan.start(lax.axis_index("tm") + 1), plan.window)
    run_copies([(heads.at[0, :, :, others], out)], sems)


def lines_kernel(plan, cells, weights, lines):
    at = 0
    for step in range(STEPS):
        place = cells[0, step : step + 1].astype(F32)
        row = jnp.floor((place + 0.5) * (1.0 / plan.width))
        lines[at : at + 1] = row
        lines[at + 1 : at + 2] = place - row * plan.width
        lines[at + 2 : at + 2 + plan.members] = weights[0, step]
        at += 2 + plan.members


def force_kernel(plan, top, count, obs, force):
    me = lax.axis_index("tm")
    tile = lax.axis_index("tile")
    start = plan.start(me)
    members, observed = (plan.members, plan.observed)
    wides = -(-plan.window // WIDE)

    def observe(number, step, low, height):
        lines = obs[(top - number) ^ me]
        first = (2 + members) * step
        row = lines[first : first + 1] - ((tile - 1) * plan.rows + low).astype(F32)
        col = lines[first + 1 : first + 2] - start.astype(F32)
        inside = (row >= 0.0) & (row < height) & (col >= 0.0) & (col < plan.window)
        group = jnp.floor(col * (1.0 / WIDE))
        key = jnp.where(inside, group * height + row, -1.0).astype(jnp.int32)
        within = (col - group * WIDE).astype(jnp.int32)
        hit = lax.broadcasted_iota(jnp.int32, (wides * height, observed), 0) == key
        left = []
        for m in range(members):
            weight = lines[first + 2 + m : first + 3 + m]
            parts = []
            for _ in range(PIECES):
                piece = weight.astype(BF16).astype(F32)
                parts.append(jnp.where(hit, piece, 0.0).astype(BF16))
                weight = weight - piece
            left.append(jnp.concatenate(parts, axis=1))
        place = lax.broadcasted_iota(jnp.int32, (WIDE, observed), 0)
        right = jnp.where(place == within, 1.0, 0.0).astype(BF16)
        found = lax.dot_general(
            jnp.concatenate(left, axis=0),
            jnp.concatenate([right] * PIECES, axis=1),
            (((1,), (1,)), ((), ())),
            preferred_element_type=F32,
        )
        for m in range(members):
            for g in range(wides):
                at = (m * wides + g) * height
                end = min(plan.window, (g + 1) * WIDE)
                value = found[at : at + height, : end - g * WIDE]
                force[number, step, m, low : low + height, g * WIDE : end] = value

    for first, end, low in plan.bands(top, count):

        def body(number, _, low=low):
            for step in range(STEPS):
                observe(number, step, low, plan.ext - 2 * low)

        lax.fori_loop(first, end, body, None)


def chain_kernel(plan, top, count, mask, packed_in, inner, outer, force, *rest):
    first = top == plan.sections - 1
    if not first:
        field, field_inner, field_outer = rest[:3]
        rest = rest[3:]
    history, mine, send, east, west, south, north, act_rd, cap_rd, x0, x1, rhs, packed, sem = rest
    copy = pltpu.make_async_copy(packed_in, packed, sem)
    copy.start()
    me = lax.axis_index("tm")
    tile = lax.axis_index("tile")
    rows, ext, members, tiles = (plan.rows, plan.ext, plan.members, plan.tiles)
    start = plan.start(me)
    even = tile % 2 == 0

    def stacked(own, core, chip, index, columns):
        a, b = (core[index, :, columns], chip[index, :, columns])
        parts = [jnp.where(even, b, a), own[index, :, columns], jnp.where(even, a, b)]
        return jnp.concatenate(parts, axis=0)

    lane = lax.broadcasted_iota(jnp.int32, (1, LANES), 1)
    ends = lane == LANES - 1
    begins = lane == 0
    tile_rows = lax.axis_size("tile") * rows

    def chunk_active(chunk, column):
        if column >= tiles:
            return jnp.float32(0.0)
        row = (tile + chunk - 1) * rows
        inside = (row >= 0) & (row < tile_rows)
        block = jnp.clip(row, 0, tile_rows - 1) // BLOCK
        value = mask[block, (start + column * LANES) // BLOCK]
        return jnp.where(inside, value, 0).astype(F32)

    def active(column):
        parts = [jnp.full((rows, LANES), chunk_active(chunk, column), F32) for chunk in range(3)]
        return jnp.concatenate(parts, axis=0)

    def cols(column):
        return pl.ds(column * LANES, LANES)

    row_id = lax.broadcasted_iota(jnp.int32, (ext, LANES), 0)
    act = active(0)
    previous = jnp.zeros((ext, LANES), F32)
    copy.wait()
    for c in range(tiles):
        act_next = active(c + 1)
        pair = act * jnp.where(ends, act_next, act)
        e = stacked(packed, inner, outer, 1, cols(c)) * pair
        w = pltpu.roll(jnp.where(ends, previous, e), 1, axis=1)
        below = jnp.where(row_id == ext - 1, 0.0, pltpu.roll(act, ext - 1, axis=0))
        s = stacked(packed, inner, outer, 2, cols(c)) * act * below
        n = jnp.where(row_id == 0, 0.0, pltpu.roll(s, 1, axis=0))
        cap = stacked(packed, inner, outer, 0, cols(c))
        diagonal = cap + e + w + s + n
        inverse = jnp.where(diagonal > 0.0, 1.0 / jnp.where(diagonal > 0.0, diagonal, 1.0), 0.0)
        east[:, cols(c)] = e * inverse
        west[:, cols(c)] = w * inverse
        south[:, cols(c)] = s * inverse
        north[:, cols(c)] = n * inverse
        act_rd[:, cols(c)] = act * inverse
        cap_rd[:, cols(c)] = act * cap * inverse
        for m in range(members):
            if first:
                x0[m, :, cols(c)] = stacked(packed, inner, outer, 3 + m, cols(c))
            else:
                x0[m, :, cols(c)] = stacked(field, field_inner, field_outer, m, cols(c))
        previous = e
        act = act_next

    def sweep(source, target, low, height, number, step, initial):
        band = slice(low, low + height)
        zero = jnp.zeros((height, LANES), F32)
        here = [source[m, band, cols(0)] for m in range(members)]
        turned = [pltpu.roll(h, LANES - 1, axis=1) for h in here]
        left = [zero] * members
        for c in range(tiles):
            e, w, s, n = (ref[band, cols(c)] for ref in (east, west, south, north))
            for m in range(members):
                if c + 1 < tiles:
                    after = source[m, band, cols(c + 1)]
                    after_turned = pltpu.roll(after, LANES - 1, axis=1)
                else:
                    after = after_turned = zero
                back = pltpu.roll(here[m], 1, axis=1)
                x_east = jnp.where(ends, after_turned, turned[m])
                x_west = jnp.where(begins, left[m], back)
                x_south = pltpu.roll(here[m], height - 1, axis=0)
                x_north = pltpu.roll(here[m], 1, axis=0)
                if initial:
                    value = cap_rd[band, cols(c)] * here[m] + act_rd[band, cols(c)] * force[number, step, m, band, cols(c)]
                    rhs[m, band, cols(c)] = value
                else:
                    value = rhs[m, band, cols(c)]
                target[m, band, cols(c)] = value + e * x_east + w * x_west + s * x_south + n * x_north
                left[m], here[m], turned[m] = (back, after, after_turned)

    lowest = me - me % 2

    def one_section(number, low):
        slot = jnp.clip(top - number - lowest, 0, 1)
        height = ext - 2 * low
        for step in reversed(range(STEPS)):
            refs = (x0, x1)
            for index in range(SWEEPS):
                sweep(refs[index % 2], refs[(index + 1) % 2], low, height, number, step, index == 0)
            if SWEEPS % 2:
                x0[:, low : low + height, :] = x1[:, low : low + height, :]
            history[slot, step] = x0[:, rows : 2 * rows, :]

    wanted = top - lowest + 1
    for begin, end, low in plan.bands(top, count):
        lax.fori_loop(begin, jnp.clip(wanted, begin, end), lambda i, _, low=low: one_section(i, low), None)

    own = pl.ds(plan.own(me), plan.half)
    mine[...] = history[me % 2, 0, :, :, own]
    send[...] = history[1 - me % 2, 0, :, :, own]


def sens_kernel(plan, mask, packed, history, heads, other_heads, *rest):
    cond_outs, storage_out = (rest[:-1], rest[-1])
    me = lax.axis_index("tm")
    tile = lax.axis_index("tile")
    rows, members = (plan.rows, plan.members)
    start, own = (plan.start(me), plan.own(me))
    side, group = (me % 2, me // 2)
    ends = lax.broadcasted_iota(jnp.int32, (1, LANES), 1) == LANES - 1
    block_row = tile * rows // BLOCK
    columns = plan.width // LANES

    def after(here, following):
        return jnp.where(ends, pltpu.roll(following, LANES - 1, axis=1), pltpu.roll(here, LANES - 1, axis=1))

    def lanes(offset):
        return pl.ds(pl.multiple_of(offset, LANES), LANES)

    stored = [jnp.zeros((rows, LANES), F32) for _ in range(members)]
    for slot, out in enumerate(cond_outs):
        for t in range(plan.out_columns // LANES):
            here = own + (group ^ slot) * plan.out_columns + t * LANES
            there = jnp.minimum(here + LANES, plan.window - LANES)
            column = (start + here) // LANES
            act = mask[block_row, column].astype(F32)
            act_next = mask[block_row, jnp.minimum(column + 1, columns - 1)].astype(F32)
            act_next = jnp.where(column + 1 < columns, act_next, 0.0)
            pair = act * jnp.where(ends, act_next, act)
            capacity = packed[0, :, lanes(here)]
            sens = jnp.zeros((rows, LANES), F32)
            for which in range(2):
                section = side if which == 0 else 1 - side
                if which == 0:
                    levels = [heads[0, k, :, lanes(start + here)] for k in range(STEPS + 1)]
                    nexts = [heads[0, k, :, lanes(start + there)] for k in range(STEPS + 1)]
                else:
                    levels = [other_heads[k, :, lanes(here)] for k in range(STEPS + 1)]
                    nexts = [other_heads[k, :, lanes(there)] for k in range(STEPS + 1)]
                for step in range(STEPS):
                    fields = [history[section, step, m, :, lanes(here)] for m in range(members)]
                    rise = capacity * (levels[step + 1] - levels[step])
                    for m in range(members):
                        stored[m] = stored[m] + fields[m] * rise
                    both = functools.reduce(jnp.add, fields)
                    follow = [history[section, step, m, :, lanes(there)] for m in range(members)]
                    both_next = functools.reduce(jnp.add, follow)
                    slope = after(levels[step + 1], nexts[step + 1]) - levels[step + 1]
                    sens = sens + (after(both, both_next) - both) * slope
            out[:, t * LANES : (t + 1) * LANES] = sens * pair
    storage_out[...] = jnp.zeros((8, LANES), F32)
    for m in range(members):
        storage_out[m : m + 1, :] = jnp.full((1, LANES), jnp.sum(stored[m]), F32)


def shards(heads, capacity, cond_row, cond_col, terminal, obs_cell, obs_weight, block_mask):
    rows, width = capacity.shape
    members = terminal.shape[0]
    sections = lax.axis_size("tm")
    plan = Plan(rows, width, sections, members, obs_cell.shape[2])
    window, ext, half = (plan.window, plan.ext, plan.half)
    me = lax.axis_index("tm")
    anywhere = pl.BlockSpec(memory_space=pl.ANY)
    in_vmem = pl.BlockSpec(memory_space=pltpu.VMEM)
    in_smem = pl.BlockSpec(memory_space=pltpu.SMEM)
    params = pltpu.CompilerParams(vmem_limit_bytes=VMEM_LIMIT)

    def shape(*dims):
        return jax.ShapeDtypeStruct(dims, F32)

    packed = pl.pallas_call(
        functools.partial(pack_kernel, plan),
        out_shape=shape(3 + members, rows, window),
        in_specs=[anywhere] * 4,
        out_specs=in_vmem,
        scratch_shapes=[pltpu.SemaphoreType.DMA((4,))],
        name="pack",
    )(capacity, cond_row, cond_col, terminal)
    head_send = pl.pallas_call(
        functools.partial(heads_kernel, plan),
        out_shape=shape(STEPS + 1, rows, window),
        in_specs=[anywhere],
        out_specs=in_vmem,
        scratch_shapes=[pltpu.SemaphoreType.DMA((1,))],
        name="heads",
    )(heads)
    lines = pl.pallas_call(
        functools.partial(lines_kernel, plan),
        out_shape=shape(STEPS * (2 + members), plan.observed),
        in_specs=[in_vmem] * 2,
        out_specs=in_vmem,
        name="lines",
    )(obs_cell, obs_weight)
    outer = outer_pairs(packed)
    inner = inner_pairs(packed)

    obs = gather(lines, "tm")
    obs, head_send = lax.optimization_barrier((obs, head_send))
    other_heads = fetch(head_send, "tm", 1)

    part = (members, rows, half)
    top = sections - 1
    field = []
    results = None
    while top >= 0:
        count = min(plan.per_phase, top + 1)
        force = pl.pallas_call(
            functools.partial(force_kernel, plan, top, count),
            out_shape=shape(count, STEPS, members, ext, window),
            in_specs=[in_vmem],
            out_specs=in_vmem,
            compiler_params=params,
            name="force",
        )(obs)
        plane = pltpu.VMEM((ext, window), F32)
        fields = pltpu.VMEM((members, ext, window), F32)
        now = pl.pallas_call(
            functools.partial(chain_kernel, plan, top, count),
            out_shape=[shape(2, STEPS, members, rows, window), shape(*part), shape(*part)],
            in_specs=[in_smem, anywhere] + [in_vmem] * (3 + len(field)),
            out_specs=[in_vmem] * 3,
            scratch_shapes=[
                *([plane] * 6),
                *([fields] * 3),
                pltpu.VMEM((3 + members, rows, window), F32),
                pltpu.SemaphoreType.DMA,
            ],
            compiler_params=params,
            name="chain",
        )(block_mask, packed, inner, outer, force, *field)
        if results is None:
            results = now
        else:
            results = [jnp.where(me - me % 2 > top, a, b) for a, b in zip(results, now)]
        top -= count
        if top >= 0:
            reached = now[0][0, 0]
            field = [reached, inner_pairs(reached), outer_pairs(reached)]
    history, mine, send = results

    other = fetch(send, "tm", 1)
    *cond, storage = pl.pallas_call(
        functools.partial(sens_kernel, plan),
        out_shape=[shape(rows, plan.out_columns)] * plan.groups + [shape(8, LANES)],
        in_specs=[in_smem] + [in_vmem] * 4,
        out_specs=[in_vmem] * (plan.groups + 1),
        compiler_params=params,
        name="sens",
    )(block_mask, packed, history, heads, other_heads)

    groups = plan.groups
    parts = []
    for slot in range(groups):
        moves = [(i, (i % 2) * groups + (i // 2 ^ slot)) for i in range(sections)]
        parts.append(lax.ppermute(cond[slot], "tm", moves))
    cond = functools.reduce(jnp.add, parts)
    storage = total(storage, "tile")
    side = me % 2
    halves = [jnp.where(side == 0, mine, other), jnp.where(side == 0, other, mine)]
    adjoint = jnp.concatenate(halves, axis=2)
    storage, adjoint = lax.optimization_barrier((storage, adjoint))
    storage = total(storage, "tm")
    return (adjoint[None], cond, storage[:members, 0])


def solution(mesh):
    placed = (
        P("tm", None, "tile", None),
        P("tile", None),
        P("tile", None),
        P("tile", None),
        P(None, "tile", None),
        P("tm", None, None),
        P("tm", None, None, None),
        P(),
    )
    return jax.shard_map(
        shards,
        mesh=mesh,
        in_specs=placed,
        out_specs=(P("tm", None, "tile", None), P("tile", "tm"), P()),
        check_vma=False,
    )
```

```python
import functools

import jax
import jax.numpy as jnp
from jax import lax
from jax.experimental import pallas as pl
from jax.experimental.pallas import tpu as pltpu
from jax.sharding import PartitionSpec as P

BLOCK = 128
STEPS = 2
SWEEPS = 2
LANES = 128
WIDE = 256
PIECES = 3
UNROLL = 32
F32 = jnp.float32
BF16 = jnp.bfloat16
VMEM_LIMIT = 24 * 2**20


def fetch(value, axis, hop):
    count = lax.axis_size(axis)
    return lax.ppermute(value, axis, [(i ^ hop, i) for i in range(count)])


def gather(value, axis):
    blocks, hop = (value[None], 1)
    while 2 * hop < lax.axis_size(axis):
        blocks = jnp.concatenate([blocks, fetch(blocks, axis, hop)], axis=0)
        hop *= 2
    return blocks, fetch(blocks, axis, hop)


def total(value, axis, hop=1, until=None):
    while hop < (until or lax.axis_size(axis)):
        value = value + fetch(value, axis, hop)
        hop *= 2
    return value


def inner_pairs(value):
    count = lax.axis_size("tile")
    pairs = [(i, i ^ 1) for i in range(count) if i ^ 1 < count]
    return lax.ppermute(value, "tile", pairs)


def outer_pairs(value):
    count = lax.axis_size("tile")
    low = range(1, count - 1, 2)
    return lax.ppermute(value, "tile", [(i, i + 1) for i in low] + [(i + 1, i) for i in low])


class Plan:
    def __init__(self, rows, width, sections, members, observed):
        self.rows, self.width, self.sections = (rows, width, sections)
        self.members, self.observed = (members, observed)
        self.half = width // 2
        sweeps = sections * STEPS * SWEEPS
        self.halo = -(-sweeps // LANES) * LANES
        self.window = self.half + self.halo
        self.tiles = self.window // LANES
        self.ext = 3 * rows
        self.per_phase = max(1, rows // (STEPS * SWEEPS))
        self.groups = sections // 2
        self.out_columns = width // sections

    def start(self, index):
        return pl.multiple_of((index % 2) * (self.half - self.halo), LANES)

    def own(self, index):
        return pl.multiple_of((index % 2) * self.halo, LANES)

    def bands(self, count):
        return [(number, number * STEPS * SWEEPS // 4 * 4) for number in range(count)]


def run_copies(copies, sems):
    started = [pltpu.make_async_copy(a, b, sems.at[i]) for i, (a, b) in enumerate(copies)]
    for copy in started:
        copy.start()
    for copy in started:
        copy.wait()


def pack_kernel(plan, capacity, cond_row, cond_col, terminal, packed, room, into, out):
    columns = pl.ds(plan.start(lax.axis_index("tm")), plan.window)
    fields = pl.ds(3, plan.members)
    parts = [(ref.at[:, columns], i) for i, ref in enumerate((capacity, cond_row, cond_col))]
    parts.append((terminal.at[:, :, columns], fields))
    loads = [pltpu.make_async_copy(ref, room.at[i], into.at[k]) for k, (ref, i) in enumerate(parts)]
    stores = [pltpu.make_async_copy(room.at[i], packed.at[i], out.at[k]) for k, (_, i) in enumerate(parts)]
    for load in loads:
        load.start()
    for load, store in zip(loads, stores):
        load.wait()
        store.start()
    for store in stores:
        store.wait()


def lines_kernel(plan, cells, weights, lines):
    at = 0
    for step in range(STEPS):
        place = cells[0, step : step + 1].astype(F32)
        row = jnp.floor((place + 0.5) * (1.0 / plan.width))
        lines[at : at + 1] = row
        lines[at + 1 : at + 2] = place - row * plan.width
        lines[at + 2 : at + 2 + plan.members] = weights[0, step]
        at += 2 + plan.members


def heads_kernel(plan, heads, out, sems):
    others = pl.ds(plan.start(lax.axis_index("tm") + 1), plan.window)
    run_copies([(heads.at[0, :, :, others], out)], sems)


def force_kernel(plan, top, count, obs_near, obs_far, force):
    me = lax.axis_index("tm")
    tile = lax.axis_index("tile")
    start = plan.start(me)
    members, observed = (plan.members, plan.observed)
    wides = -(-plan.window // WIDE)

    def observe(number, step, low, height):
        block = (top - number) ^ me
        split = plan.sections // 2
        near = obs_near[jnp.minimum(block, split - 1)]
        lines = jnp.where(block < split, near, obs_far[jnp.maximum(block - split, 0)])
        first = (2 + members) * step
        row = lines[first : first + 1] - ((tile - 1) * plan.rows + low).astype(F32)
        col = lines[first + 1 : first + 2] - start.astype(F32)
        inside = (row >= 0.0) & (row < height) & (col >= 0.0) & (col < plan.window)
        group = jnp.floor(col * (1.0 / WIDE))
        key = jnp.where(inside, group * height + row, -1.0).astype(jnp.int32)
        within = (col - group * WIDE).astype(jnp.int32)
        hit = lax.broadcasted_iota(jnp.int32, (wides * height, observed), 0) == key
        left = []
        for m in range(members):
            weight = lines[first + 2 + m : first + 3 + m]
            parts = []
            for _ in range(PIECES):
                piece = weight.astype(BF16).astype(F32)
                parts.append(jnp.where(hit, piece, 0.0).astype(BF16))
                weight = weight - piece
            left.append(jnp.concatenate(parts, axis=1))
        place = lax.broadcasted_iota(jnp.int32, (WIDE, observed), 0)
        right = jnp.where(place == within, 1.0, 0.0).astype(BF16)
        found = lax.dot_general(
            jnp.concatenate(left, axis=0),
            jnp.concatenate([right] * PIECES, axis=1),
            (((1,), (1,)), ((), ())),
            preferred_element_type=F32,
        )
        for m in range(members):
            for t in range(plan.tiles):
                at = (m * wides + t * LANES // WIDE) * height
                lane = t * LANES % WIDE
                force[number, step, m, t, :height, :] = found[at : at + height, lane : lane + LANES]

    for number, low in plan.bands(count):
        for step in range(STEPS):
            observe(number, step, low, plan.ext - 2 * low)


def chain_kernel(plan, top, count, mask, packed_in, inner, outer, force, *rest):
    first = top == plan.sections - 1
    if not first:
        field, field_inner, field_outer = rest[:3]
        rest = rest[3:]
    history, mine, send, own_capacity, east, west, south, north, act_rd, cap_rd, x0, x1, rhs, packed, sem = rest
    copy = pltpu.make_async_copy(packed_in, packed, sem)
    copy.start()
    me = lax.axis_index("tm")
    tile = lax.axis_index("tile")
    rows, ext, members, tiles = (plan.rows, plan.ext, plan.members, plan.tiles)
    start = plan.start(me)
    even = tile % 2 == 0

    def stacked(own, core, chip, index, columns):
        a, b = (core[index, :, columns], chip[index, :, columns])
        parts = [jnp.where(even, b, a), own[index, :, columns], jnp.where(even, a, b)]
        return jnp.concatenate(parts, axis=0)

    lane = lax.broadcasted_iota(jnp.int32, (1, LANES), 1)
    ends = lane == LANES - 1
    begins = lane == 0
    tile_rows = lax.axis_size("tile") * rows

    def chunk_active(chunk, column):
        if column >= tiles:
            return jnp.float32(0.0)
        row = (tile + chunk - 1) * rows
        inside = (row >= 0) & (row < tile_rows)
        block = jnp.clip(row, 0, tile_rows - 1) // BLOCK
        value = mask[block, (start + column * LANES) // BLOCK]
        return jnp.where(inside, value, 0).astype(F32)

    def active(column):
        parts = [jnp.full((rows, LANES), chunk_active(chunk, column), F32) for chunk in range(3)]
        return jnp.concatenate(parts, axis=0)

    def cols(column):
        return pl.ds(column * LANES, LANES)

    row_id = lax.broadcasted_iota(jnp.int32, (ext, LANES), 0)
    act = active(0)
    previous = jnp.zeros((ext, LANES), F32)
    copy.wait()
    own_capacity[...] = packed[0]
    for c in range(tiles):
        act_next = active(c + 1)
        pair = act * jnp.where(ends, act_next, act)
        e = stacked(packed, inner, outer, 1, cols(c)) * pair
        w = pltpu.roll(jnp.where(ends, previous, e), 1, axis=1)
        below = jnp.where(row_id == ext - 1, 0.0, pltpu.roll(act, ext - 1, axis=0))
        s = stacked(packed, inner, outer, 2, cols(c)) * act * below
        n = jnp.where(row_id == 0, 0.0, pltpu.roll(s, 1, axis=0))
        cap = stacked(packed, inner, outer, 0, cols(c))
        diagonal = cap + e + w + s + n
        inverse = jnp.where(diagonal > 0.0, 1.0 / jnp.where(diagonal > 0.0, diagonal, 1.0), 0.0)
        east[c] = e * inverse
        west[c] = w * inverse
        south[c] = s * inverse
        north[c] = n * inverse
        act_rd[c] = act * inverse
        cap_rd[c] = act * cap * inverse
        for m in range(members):
            if first:
                x0[m, c] = stacked(packed, inner, outer, 3 + m, cols(c))
            else:
                x0[m, c] = stacked(field, field_inner, field_outer, m, cols(c))
        previous = e
        act = act_next

    def sweep(source, target, low, number, step, initial):
        depth = (ext - 2 * low) // 8
        every = range(depth)
        pairs = [(m, v) for m in range(members) for v in every]

        def rows_of(v, first=low):
            return pl.ds(first + v, 8, stride=depth)

        def load(c):
            return [source[m, c, rows_of(v), :] for m, v in pairs]

        def group(first, length):
            before = load(first - 1) if not isinstance(first, int) or first else None
            here = load(first)
            for c in [first + i for i in range(length)]:
                after = load(c + 1) if not isinstance(c, int) or c + 1 < tiles else here
                before = before or here
                for v in every:
                    e, w, s, n = (ref[c, rows_of(v), :] for ref in (east, west, south, north))
                    if initial:
                        a, k = (act_rd[c, rows_of(v), :], cap_rd[c, rows_of(v), :])
                    for m in range(members):
                        at = m * depth + v
                        x = here[m * depth : (m + 1) * depth]
                        x_east = pltpu.roll(jnp.where(begins, after[at], x[v]), LANES - 1, axis=1)
                        x_west = pltpu.roll(jnp.where(ends, before[at], x[v]), 1, axis=1)
                        x_south = x[v + 1] if v + 1 < depth else pltpu.roll(x[0], 7, axis=0)
                        x_north = x[v - 1] if v else pltpu.roll(x[depth - 1], 1, axis=0)
                        if initial:
                            value = k * x[v] + a * force[number, step, m, c, rows_of(v, 0), :]
                            rhs[m, c, rows_of(v), :] = value
                        else:
                            value = rhs[m, c, rows_of(v), :]
                        value = value + e * x_east + w * x_west + s * x_south + n * x_north
                        target[m, c, rows_of(v), :] = value
                before, here = (here, after)

        if UNROLL >= tiles:
            group(0, tiles)
        else:
            group(0, 1)
            turns = (tiles - 2) // UNROLL
            lax.fori_loop(0, turns, lambda i, _: group(i * UNROLL + 1, UNROLL), None)
            group(1 + turns * UNROLL, tiles - 1 - turns * UNROLL)

    lowest = me - me % 2

    def one_section(number, low):
        slot = jnp.clip(top - number - lowest, 0, 1)
        for step in reversed(range(STEPS)):
            refs = (x0, x1)
            for index in range(SWEEPS):
                sweep(refs[index % 2], refs[(index + 1) % 2], low, number, step, index == 0)
            if SWEEPS % 2:
                x0[...] = x1[...]

            @pl.when(top - number - lowest < 2)
            def _():
                for c in range(tiles):
                    history[slot, step, :, :, cols(c)] = x0[:, c, rows : 2 * rows, :]

    for number, low in plan.bands(count):
        pl.when(top - number >= lowest)(functools.partial(one_section, number, low))

    own = pl.ds(plan.own(me), plan.half)
    mine[...] = history[me % 2, 0, :, :, own]
    send[...] = history[1 - me % 2, 0, :, :, own]


def window_of_heads(plan, heads, other_heads, step, columns, which):
    if which:
        return other_heads[step, :, columns]
    start = plan.start(lax.axis_index("tm"))
    return heads[0, step, :, pl.ds(pl.multiple_of(start + columns.start, LANES), columns.size)]


def storage_kernel(plan, own_capacity, history, heads, other_heads, out):
    me = lax.axis_index("tm")
    members = plan.members
    stored = [jnp.zeros((plan.rows, LANES), F32) for _ in range(members)]
    for t in range(plan.half // LANES):
        here = pl.ds(pl.multiple_of(plan.own(me) + t * LANES, LANES), LANES)
        capacity = own_capacity[:, here]
        for which in range(2):
            section = me % 2 if which == 0 else 1 - me % 2
            levels = [window_of_heads(plan, heads, other_heads, k, here, which) for k in range(STEPS + 1)]
            for step in range(STEPS):
                rise = capacity * (levels[step + 1] - levels[step])
                for m in range(members):
                    stored[m] = stored[m] + history[section, step, m, :, here] * rise
    out[...] = jnp.zeros((8, LANES), F32)
    for m in range(members):
        out[m : m + 1, :] = jnp.full((1, LANES), jnp.sum(stored[m]), F32)


def cond_kernel(plan, mask, history, heads, other_heads, *outs):
    me = lax.axis_index("tm")
    tile = lax.axis_index("tile")
    rows, members = (plan.rows, plan.members)
    start, own = (plan.start(me), plan.own(me))
    side, group = (me % 2, me // 2)
    ends = lax.broadcasted_iota(jnp.int32, (1, LANES), 1) == LANES - 1
    block_row = tile * rows // BLOCK
    columns = plan.width // LANES

    def after(here, following):
        return jnp.where(ends, pltpu.roll(following, LANES - 1, axis=1), pltpu.roll(here, LANES - 1, axis=1))

    def lanes(offset):
        return pl.ds(pl.multiple_of(offset, LANES), LANES)

    for slot, out in enumerate(outs):
        for t in range(plan.out_columns // LANES):
            here = own + (group ^ slot) * plan.out_columns + t * LANES
            there = jnp.minimum(here + LANES, plan.window - LANES)
            column = (start + here) // LANES
            act = mask[block_row, column].astype(F32)
            act_next = mask[block_row, jnp.minimum(column + 1, columns - 1)].astype(F32)
            act_next = jnp.where(column + 1 < columns, act_next, 0.0)
            pair = act * jnp.where(ends, act_next, act)
            sens = jnp.zeros((rows, LANES), F32)
            for which in range(2):
                section = side if which == 0 else 1 - side
                for step in range(STEPS):
                    level = window_of_heads(plan, heads, other_heads, step + 1, lanes(here), which)
                    level_next = window_of_heads(plan, heads, other_heads, step + 1, lanes(there), which)
                    both = functools.reduce(jnp.add, [history[section, step, m, :, lanes(here)] for m in range(members)])
                    follow = [history[section, step, m, :, lanes(there)] for m in range(members)]
                    both_next = functools.reduce(jnp.add, follow)
                    sens = sens + (after(both, both_next) - both) * (after(level, level_next) - level)
            out[:, t * LANES : (t + 1) * LANES] = sens * pair


def shards(heads, capacity, cond_row, cond_col, terminal, obs_cell, obs_weight, block_mask):
    rows, width = capacity.shape
    members = terminal.shape[0]
    sections = lax.axis_size("tm")
    plan = Plan(rows, width, sections, members, obs_cell.shape[2])
    window, ext, half = (plan.window, plan.ext, plan.half)
    me = lax.axis_index("tm")
    anywhere = pl.BlockSpec(memory_space=pl.ANY)
    in_vmem = pl.BlockSpec(memory_space=pltpu.VMEM)
    in_smem = pl.BlockSpec(memory_space=pltpu.SMEM)
    params = pltpu.CompilerParams(vmem_limit_bytes=VMEM_LIMIT)

    def shape(*dims):
        return jax.ShapeDtypeStruct(dims, F32)

    packed = pl.pallas_call(
        functools.partial(pack_kernel, plan),
        out_shape=shape(3 + members, rows, window),
        in_specs=[anywhere] * 4,
        out_specs=anywhere,
        scratch_shapes=[
            pltpu.VMEM((3 + members, rows, window), F32),
            pltpu.SemaphoreType.DMA((4,)),
            pltpu.SemaphoreType.DMA((4,)),
        ],
        name="pack",
    )(capacity, cond_row, cond_col, terminal)
    later_weight, _ = lax.optimization_barrier((obs_weight, packed))
    lines = pl.pallas_call(
        functools.partial(lines_kernel, plan),
        out_shape=shape(STEPS * (2 + members), plan.observed),
        in_specs=[in_vmem] * 2,
        out_specs=in_vmem,
        name="lines",
    )(obs_cell, later_weight)
    head_send = pl.pallas_call(
        functools.partial(heads_kernel, plan),
        out_shape=shape(STEPS + 1, rows, window),
        in_specs=[anywhere],
        out_specs=in_vmem,
        scratch_shapes=[pltpu.SemaphoreType.DMA((1,))],
        name="heads",
    )(heads)
    outer = outer_pairs(packed)
    inner = inner_pairs(packed)
    lines, inner = lax.optimization_barrier((lines, inner))
    obs = gather(lines, "tm")
    *obs, head_send = lax.optimization_barrier((*obs, head_send))
    other_heads = fetch(head_send, "tm", 1)

    part = (members, rows, half)
    top = sections - 1
    field = []
    results = None
    while top >= 0:
        count = min(plan.per_phase, top + 1)
        force = pl.pallas_call(
            functools.partial(force_kernel, plan, top, count),
            out_shape=shape(count, STEPS, members, plan.tiles, ext, LANES),
            in_specs=[in_vmem] * 2,
            out_specs=in_vmem,
            compiler_params=params,
            name="force",
        )(*obs)
        plane = pltpu.VMEM((plan.tiles, ext, LANES), F32)
        fields = pltpu.VMEM((members, plan.tiles, ext, LANES), F32)
        now = pl.pallas_call(
            functools.partial(chain_kernel, plan, top, count),
            out_shape=[shape(2, STEPS, members, rows, window), shape(*part), shape(*part), shape(rows, window)],
            in_specs=[in_smem, anywhere] + [in_vmem] * (3 + len(field)),
            out_specs=[in_vmem] * 4,
            scratch_shapes=[
                *([plane] * 6),
                *([fields] * 3),
                pltpu.VMEM((3 + members, rows, window), F32),
                pltpu.SemaphoreType.DMA,
            ],
            compiler_params=params,
            name="chain",
        )(block_mask, packed, inner, outer, force, *field)
        if results is None:
            results = now
        else:
            results = [jnp.where(me - me % 2 > top, a, b) for a, b in zip(results, now)]
        top -= count
        if top >= 0:
            reached = now[0][0, 0]
            field = [reached, inner_pairs(reached), outer_pairs(reached)]
    history, mine, send, own_capacity = results

    storage = pl.pallas_call(
        functools.partial(storage_kernel, plan),
        out_shape=shape(8, LANES),
        in_specs=[in_vmem] * 4,
        out_specs=in_vmem,
        compiler_params=params,
        name="storage",
    )(own_capacity, history, heads, other_heads)
    storage, send = lax.optimization_barrier((storage, send))
    other = fetch(send, "tm", 1)
    cond = pl.pallas_call(
        functools.partial(cond_kernel, plan),
        out_shape=[shape(rows, plan.out_columns)] * plan.groups,
        in_specs=[in_smem] + [in_vmem] * 3,
        out_specs=[in_vmem] * plan.groups,
        compiler_params=params,
        name="cond",
    )(block_mask, history, heads, other_heads)

    storage = total(storage, "tile", until=4)
    storage, *cond = lax.optimization_barrier((storage, *cond))
    groups = plan.groups
    parts = []
    for slot in range(groups):
        moves = [(i, (i % 2) * groups + (i // 2 ^ slot)) for i in range(sections)]
        parts.append(lax.ppermute(cond[slot], "tm", moves))
    storage = total(storage, "tile", hop=4)
    storage = total(storage, "tm", until=2)
    side = me % 2
    halves = [jnp.where(side == 0, mine, other), jnp.where(side == 0, other, mine)]
    adjoint = jnp.concatenate(halves, axis=2)
    storage, adjoint = lax.optimization_barrier((storage, adjoint))
    storage = total(storage, "tm", hop=2)
    cond = functools.reduce(jnp.add, parts)
    return (adjoint[None], cond, storage[:members, 0])


def solution(mesh):
    placed = (
        P("tm", None, "tile", None),
        P("tile", None),
        P("tile", None),
        P("tile", None),
        P(None, "tile", None),
        P("tm", None, None),
        P("tm", None, None, None),
        P(),
    )
    return jax.shard_map(
        shards,
        mesh=mesh,
        in_specs=placed,
        out_specs=(P("tm", None, "tile", None), P("tile", "tm"), P()),
        check_vma=False,
    )
```

```python
import functools

import jax
import jax.numpy as jnp
from jax import lax
from jax.experimental import pallas as pl
from jax.experimental.pallas import tpu as pltpu
from jax.sharding import PartitionSpec as P

BLOCK = 128
STEPS = 2
SWEEPS = 2
LANES = 128
WIDE = 256
PIECES = 3
UNROLL = 32
F32 = jnp.float32
BF16 = jnp.bfloat16
VMEM_LIMIT = 24 * 2**20


def fetch(value, axis, hop):
    count = lax.axis_size(axis)
    return lax.ppermute(value, axis, [(i ^ hop, i) for i in range(count)])


def gather(value, axis):
    blocks, hop = (value[None], 1)
    while 2 * hop < lax.axis_size(axis):
        blocks = jnp.concatenate([blocks, fetch(blocks, axis, hop)], axis=0)
        hop *= 2
    return blocks, fetch(blocks, axis, hop)


def total(value, axis, hop=1, until=None):
    while hop < (until or lax.axis_size(axis)):
        value = value + fetch(value, axis, hop)
        hop *= 2
    return value


def inner_pairs(value):
    count = lax.axis_size("tile")
    pairs = [(i, i ^ 1) for i in range(count) if i ^ 1 < count]
    return lax.ppermute(value, "tile", pairs)


def outer_pairs(value):
    count = lax.axis_size("tile")
    low = range(1, count - 1, 2)
    return lax.ppermute(value, "tile", [(i, i + 1) for i in low] + [(i + 1, i) for i in low])


class Plan:
    def __init__(self, rows, width, sections, members, observed):
        self.rows, self.width, self.sections = (rows, width, sections)
        self.members, self.observed = (members, observed)
        self.half = width // 2
        sweeps = sections * STEPS * SWEEPS
        self.halo = -(-sweeps // LANES) * LANES
        self.window = self.half + self.halo
        self.tiles = self.window // LANES
        self.ext = 3 * rows
        self.per_phase = max(1, rows // (STEPS * SWEEPS))
        self.groups = sections // 2
        self.out_columns = width // sections

    def start(self, index):
        return pl.multiple_of((index % 2) * (self.half - self.halo), LANES)

    def own(self, index):
        return pl.multiple_of((index % 2) * self.halo, LANES)

    def bands(self, count):
        return [(number, number * STEPS * SWEEPS // 4 * 4) for number in range(count)]


def run_copies(copies, sems):
    started = [pltpu.make_async_copy(a, b, sems.at[i]) for i, (a, b) in enumerate(copies)]
    for copy in started:
        copy.start()
    for copy in started:
        copy.wait()


def pack_kernel(plan, capacity, cond_row, cond_col, terminal, packed, room, into, out):
    columns = pl.ds(plan.start(lax.axis_index("tm")), plan.window)
    fields = pl.ds(3, plan.members)
    parts = [(ref.at[:, columns], i) for i, ref in enumerate((capacity, cond_row, cond_col))]
    parts.append((terminal.at[:, :, columns], fields))
    loads = [pltpu.make_async_copy(ref, room.at[i], into.at[k]) for k, (ref, i) in enumerate(parts)]
    stores = [pltpu.make_async_copy(room.at[i], packed.at[i], out.at[k]) for k, (_, i) in enumerate(parts)]
    for load in loads:
        load.start()
    for load, store in zip(loads, stores):
        load.wait()
        store.start()
    for store in stores:
        store.wait()


def lines_kernel(plan, cells, weights, lines):
    at = 0
    for step in range(STEPS):
        place = cells[0, step : step + 1].astype(F32)
        row = jnp.floor((place + 0.5) * (1.0 / plan.width))
        lines[at : at + 1] = row
        lines[at + 1 : at + 2] = place - row * plan.width
        lines[at + 2 : at + 2 + plan.members] = weights[0, step]
        at += 2 + plan.members


def heads_kernel(plan, heads, out, sems):
    others = pl.ds(plan.start(lax.axis_index("tm") + 1), plan.window)
    run_copies([(heads.at[0, :, :, others], out)], sems)


def force_kernel(plan, top, count, obs_near, obs_far, force):
    me = lax.axis_index("tm")
    tile = lax.axis_index("tile")
    start = plan.start(me)
    members, observed = (plan.members, plan.observed)
    wides = -(-plan.window // WIDE)

    def observe(number, step, low, height):
        block = (top - number) ^ me
        split = plan.sections // 2
        near = obs_near[jnp.minimum(block, split - 1)]
        lines = jnp.where(block < split, near, obs_far[jnp.maximum(block - split, 0)])
        first = (2 + members) * step
        row = lines[first : first + 1] - ((tile - 1) * plan.rows + low).astype(F32)
        col = lines[first + 1 : first + 2] - start.astype(F32)
        inside = (row >= 0.0) & (row < height) & (col >= 0.0) & (col < plan.window)
        group = jnp.floor(col * (1.0 / WIDE))
        key = jnp.where(inside, group * height + row, -1.0).astype(jnp.int32)
        within = (col - group * WIDE).astype(jnp.int32)
        hit = lax.broadcasted_iota(jnp.int32, (wides * height, observed), 0) == key
        left = []
        for m in range(members):
            weight = lines[first + 2 + m : first + 3 + m]
            parts = []
            for _ in range(PIECES):
                piece = weight.astype(BF16).astype(F32)
                parts.append(jnp.where(hit, piece, 0.0).astype(BF16))
                weight = weight - piece
            left.append(jnp.concatenate(parts, axis=1))
        place = lax.broadcasted_iota(jnp.int32, (WIDE, observed), 0)
        right = jnp.where(place == within, 1.0, 0.0).astype(BF16)
        found = lax.dot_general(
            jnp.concatenate(left, axis=0),
            jnp.concatenate([right] * PIECES, axis=1),
            (((1,), (1,)), ((), ())),
            preferred_element_type=F32,
        )
        for m in range(members):
            for t in range(plan.tiles):
                at = (m * wides + t * LANES // WIDE) * height
                lane = t * LANES % WIDE
                force[number, step, m, t, :height, :] = found[at : at + height, lane : lane + LANES]

    for number, low in plan.bands(count):
        for step in range(STEPS):
            observe(number, step, low, plan.ext - 2 * low)


def chain_kernel(plan, top, count, mask, packed_in, inner, outer, force, *rest):
    first = top == plan.sections - 1
    if not first:
        field, field_inner, field_outer = rest[:3]
        rest = rest[3:]
    history, mine, send, own_capacity, east, west, south, north, act_rd, cap_rd, x0, x1, rhs, packed, sem = rest
    copy = pltpu.make_async_copy(packed_in, packed, sem)
    copy.start()
    me = lax.axis_index("tm")
    tile = lax.axis_index("tile")
    rows, ext, members, tiles = (plan.rows, plan.ext, plan.members, plan.tiles)
    start = plan.start(me)
    even = tile % 2 == 0

    def stacked(own, core, chip, index, columns):
        a, b = (core[index, :, columns], chip[index, :, columns])
        parts = [jnp.where(even, b, a), own[index, :, columns], jnp.where(even, a, b)]
        return jnp.concatenate(parts, axis=0)

    lane = lax.broadcasted_iota(jnp.int32, (1, LANES), 1)
    ends = lane == LANES - 1
    begins = lane == 0
    tile_rows = lax.axis_size("tile") * rows

    def chunk_active(chunk, column):
        if column >= tiles:
            return jnp.float32(0.0)
        row = (tile + chunk - 1) * rows
        inside = (row >= 0) & (row < tile_rows)
        block = jnp.clip(row, 0, tile_rows - 1) // BLOCK
        value = mask[block, (start + column * LANES) // BLOCK]
        return jnp.where(inside, value, 0).astype(F32)

    def active(column):
        parts = [jnp.full((rows, LANES), chunk_active(chunk, column), F32) for chunk in range(3)]
        return jnp.concatenate(parts, axis=0)

    def cols(column):
        return pl.ds(column * LANES, LANES)

    row_id = lax.broadcasted_iota(jnp.int32, (ext, LANES), 0)
    act = active(0)
    previous = jnp.zeros((ext, LANES), F32)
    copy.wait()
    own_capacity[...] = packed[0]
    for c in range(tiles):
        act_next = active(c + 1)
        pair = act * jnp.where(ends, act_next, act)
        e = stacked(packed, inner, outer, 1, cols(c)) * pair
        w = pltpu.roll(jnp.where(ends, previous, e), 1, axis=1)
        below = jnp.where(row_id == ext - 1, 0.0, pltpu.roll(act, ext - 1, axis=0))
        s = stacked(packed, inner, outer, 2, cols(c)) * act * below
        n = jnp.where(row_id == 0, 0.0, pltpu.roll(s, 1, axis=0))
        cap = stacked(packed, inner, outer, 0, cols(c))
        diagonal = cap + e + w + s + n
        inverse = jnp.where(diagonal > 0.0, 1.0 / jnp.where(diagonal > 0.0, diagonal, 1.0), 0.0)
        east[c] = e * inverse
        west[c] = w * inverse
        south[c] = s * inverse
        north[c] = n * inverse
        act_rd[c] = act * inverse
        cap_rd[c] = act * cap * inverse
        for m in range(members):
            if first:
                x0[m, c] = stacked(packed, inner, outer, 3 + m, cols(c))
            else:
                x0[m, c] = stacked(field, field_inner, field_outer, m, cols(c))
        previous = e
        act = act_next

    def sweep(source, target, low, number, step, initial):
        depth = (ext - 2 * low) // 8
        every = range(depth)
        pairs = [(m, v) for m in range(members) for v in every]

        def rows_of(v, first=low):
            return pl.ds(first + v, 8, stride=depth)

        def load(c):
            return [source[m, c, rows_of(v), :] for m, v in pairs]

        def group(first, length):
            before = load(first - 1) if not isinstance(first, int) or first else None
            here = load(first)
            for c in [first + i for i in range(length)]:
                after = load(c + 1) if not isinstance(c, int) or c + 1 < tiles else here
                before = before or here
                for v in every:
                    e, w, s, n = (ref[c, rows_of(v), :] for ref in (east, west, south, north))
                    if initial:
                        a, k = (act_rd[c, rows_of(v), :], cap_rd[c, rows_of(v), :])
                    for m in range(members):
                        at = m * depth + v
                        x = here[m * depth : (m + 1) * depth]
                        x_east = pltpu.roll(jnp.where(begins, after[at], x[v]), LANES - 1, axis=1)
                        x_west = pltpu.roll(jnp.where(ends, before[at], x[v]), 1, axis=1)
                        x_south = x[v + 1] if v + 1 < depth else pltpu.roll(x[0], 7, axis=0)
                        x_north = x[v - 1] if v else pltpu.roll(x[depth - 1], 1, axis=0)
                        if initial:
                            value = k * x[v] + a * force[number, step, m, c, rows_of(v, 0), :]
                            rhs[m, c, rows_of(v), :] = value
                        else:
                            value = rhs[m, c, rows_of(v), :]
                        value = value + e * x_east + w * x_west + s * x_south + n * x_north
                        target[m, c, rows_of(v), :] = value
                before, here = (here, after)

        if UNROLL >= tiles:
            group(0, tiles)
        else:
            group(0, 1)
            turns = (tiles - 2) // UNROLL
            lax.fori_loop(0, turns, lambda i, _: group(i * UNROLL + 1, UNROLL), None)
            group(1 + turns * UNROLL, tiles - 1 - turns * UNROLL)

    lowest = me - me % 2

    def one_section(number, low):
        slot = jnp.clip(top - number - lowest, 0, 1)
        for step in reversed(range(STEPS)):
            refs = (x0, x1)
            for index in range(SWEEPS):
                sweep(refs[index % 2], refs[(index + 1) % 2], low, number, step, index == 0)
            if SWEEPS % 2:
                x0[...] = x1[...]

            @pl.when(top - number - lowest < 2)
            def _():
                for c in range(tiles):
                    history[slot, step, :, :, cols(c)] = x0[:, c, rows : 2 * rows, :]

    for number, low in plan.bands(count):
        pl.when(top - number >= lowest)(functools.partial(one_section, number, low))

    own = pl.ds(plan.own(me), plan.half)
    mine[...] = history[me % 2, 0, :, :, own]
    send[...] = history[1 - me % 2, 0, :, :, own]


def window_of_heads(plan, heads, other_heads, step, columns, which):
    if which:
        return other_heads[step, :, columns]
    start = plan.start(lax.axis_index("tm"))
    return heads[0, step, :, pl.ds(pl.multiple_of(start + columns.start, LANES), columns.size)]


def storage_kernel(plan, own_capacity, history, heads, other_heads, out):
    me = lax.axis_index("tm")
    members = plan.members
    stored = [jnp.zeros((plan.rows, LANES), F32) for _ in range(members)]
    for t in range(plan.half // LANES):
        here = pl.ds(pl.multiple_of(plan.own(me) + t * LANES, LANES), LANES)
        capacity = own_capacity[:, here]
        for which in range(2):
            section = me % 2 if which == 0 else 1 - me % 2
            levels = [window_of_heads(plan, heads, other_heads, k, here, which) for k in range(STEPS + 1)]
            for step in range(STEPS):
                rise = capacity * (levels[step + 1] - levels[step])
                for m in range(members):
                    stored[m] = stored[m] + history[section, step, m, :, here] * rise
    out[...] = jnp.zeros((8, LANES), F32)
    for m in range(members):
        out[m : m + 1, :] = jnp.full((1, LANES), jnp.sum(stored[m]), F32)


def cond_kernel(plan, mask, history, heads, other_heads, *outs):
    me = lax.axis_index("tm")
    tile = lax.axis_index("tile")
    rows, members = (plan.rows, plan.members)
    start, own = (plan.start(me), plan.own(me))
    side, group = (me % 2, me // 2)
    ends = lax.broadcasted_iota(jnp.int32, (1, LANES), 1) == LANES - 1
    block_row = tile * rows // BLOCK
    columns = plan.width // LANES

    def after(here, following):
        return jnp.where(ends, pltpu.roll(following, LANES - 1, axis=1), pltpu.roll(here, LANES - 1, axis=1))

    def lanes(offset):
        return pl.ds(pl.multiple_of(offset, LANES), LANES)

    for slot, out in enumerate(outs):
        for t in range(plan.out_columns // LANES):
            here = own + (group ^ slot) * plan.out_columns + t * LANES
            there = jnp.minimum(here + LANES, plan.window - LANES)
            column = (start + here) // LANES
            act = mask[block_row, column].astype(F32)
            act_next = mask[block_row, jnp.minimum(column + 1, columns - 1)].astype(F32)
            act_next = jnp.where(column + 1 < columns, act_next, 0.0)
            pair = act * jnp.where(ends, act_next, act)
            sens = jnp.zeros((rows, LANES), F32)
            for which in range(2):
                section = side if which == 0 else 1 - side
                for step in range(STEPS):
                    level = window_of_heads(plan, heads, other_heads, step + 1, lanes(here), which)
                    level_next = window_of_heads(plan, heads, other_heads, step + 1, lanes(there), which)
                    both = functools.reduce(jnp.add, [history[section, step, m, :, lanes(here)] for m in range(members)])
                    follow = [history[section, step, m, :, lanes(there)] for m in range(members)]
                    both_next = functools.reduce(jnp.add, follow)
                    sens = sens + (after(both, both_next) - both) * (after(level, level_next) - level)
            out[:, t * LANES : (t + 1) * LANES] = sens * pair


def shards(heads, capacity, cond_row, cond_col, terminal, obs_cell, obs_weight, block_mask):
    rows, width = capacity.shape
    members = terminal.shape[0]
    sections = lax.axis_size("tm")
    plan = Plan(rows, width, sections, members, obs_cell.shape[2])
    window, ext, half = (plan.window, plan.ext, plan.half)
    me = lax.axis_index("tm")
    anywhere = pl.BlockSpec(memory_space=pl.ANY)
    in_vmem = pl.BlockSpec(memory_space=pltpu.VMEM)
    in_smem = pl.BlockSpec(memory_space=pltpu.SMEM)
    params = pltpu.CompilerParams(vmem_limit_bytes=VMEM_LIMIT)

    def shape(*dims):
        return jax.ShapeDtypeStruct(dims, F32)

    packed = pl.pallas_call(
        functools.partial(pack_kernel, plan),
        out_shape=shape(3 + members, rows, window),
        in_specs=[anywhere] * 4,
        out_specs=anywhere,
        scratch_shapes=[
            pltpu.VMEM((3 + members, rows, window), F32),
            pltpu.SemaphoreType.DMA((4,)),
            pltpu.SemaphoreType.DMA((4,)),
        ],
        name="pack",
    )(capacity, cond_row, cond_col, terminal)
    later_weight, _ = lax.optimization_barrier((obs_weight, packed))
    lines = pl.pallas_call(
        functools.partial(lines_kernel, plan),
        out_shape=shape(STEPS * (2 + members), plan.observed),
        in_specs=[in_vmem] * 2,
        out_specs=in_vmem,
        name="lines",
    )(obs_cell, later_weight)
    head_send = pl.pallas_call(
        functools.partial(heads_kernel, plan),
        out_shape=shape(STEPS + 1, rows, window),
        in_specs=[anywhere],
        out_specs=in_vmem,
        scratch_shapes=[pltpu.SemaphoreType.DMA((1,))],
        name="heads",
    )(heads)
    outer = outer_pairs(packed)
    inner = inner_pairs(packed)
    lines, inner = lax.optimization_barrier((lines, inner))
    obs = gather(lines, "tm")
    *obs, head_send = lax.optimization_barrier((*obs, head_send))
    other_heads = fetch(head_send, "tm", 1)

    part = (members, rows, half)
    top = sections - 1
    field = []
    results = None
    while top >= 0:
        count = min(plan.per_phase, top + 1)
        force = pl.pallas_call(
            functools.partial(force_kernel, plan, top, count),
            out_shape=shape(count, STEPS, members, plan.tiles, ext, LANES),
            in_specs=[in_vmem] * 2,
            out_specs=in_vmem,
            compiler_params=params,
            name="force",
        )(*obs)
        plane = pltpu.VMEM((plan.tiles, ext, LANES), F32)
        fields = pltpu.VMEM((members, plan.tiles, ext, LANES), F32)
        now = pl.pallas_call(
            functools.partial(chain_kernel, plan, top, count),
            out_shape=[shape(2, STEPS, members, rows, window), shape(*part), shape(*part), shape(rows, window)],
            in_specs=[in_smem, anywhere] + [in_vmem] * (3 + len(field)),
            out_specs=[in_vmem] * 4,
            scratch_shapes=[
                *([plane] * 6),
                *([fields] * 3),
                pltpu.VMEM((3 + members, rows, window), F32),
                pltpu.SemaphoreType.DMA,
            ],
            compiler_params=params,
            name="chain",
        )(block_mask, packed, inner, outer, force, *field)
        if results is None:
            results = now
        else:
            results = [jnp.where(me - me % 2 > top, a, b) for a, b in zip(results, now)]
        top -= count
        if top >= 0:
            reached = now[0][0, 0]
            field = [reached, inner_pairs(reached), outer_pairs(reached)]
    history, mine, send, own_capacity = results

    storage = pl.pallas_call(
        functools.partial(storage_kernel, plan),
        out_shape=shape(8, LANES),
        in_specs=[in_vmem] * 4,
        out_specs=in_vmem,
        compiler_params=params,
        name="storage",
    )(own_capacity, history, heads, other_heads)
    storage, send = lax.optimization_barrier((storage, send))
    other = fetch(send, "tm", 1)
    cond = pl.pallas_call(
        functools.partial(cond_kernel, plan),
        out_shape=[shape(rows, plan.out_columns)] * plan.groups,
        in_specs=[in_smem] + [in_vmem] * 3,
        out_specs=[in_vmem] * plan.groups,
        compiler_params=params,
        name="cond",
    )(block_mask, history, heads, other_heads)

    storage = total(storage, "tile", until=4)
    storage, *cond = lax.optimization_barrier((storage, *cond))
    groups = plan.groups
    parts = []
    for slot in range(groups):
        moves = [(i, (i % 2) * groups + (i // 2 ^ slot)) for i in range(sections)]
        parts.append(lax.ppermute(cond[slot], "tm", moves))
    storage = total(storage, "tile", hop=4)
    storage = total(storage, "tm", until=2)
    storage, other = lax.optimization_barrier((storage, other))
    storage = total(storage, "tm", hop=2)
    mine, other, parts[0] = lax.optimization_barrier((mine, other, parts[0]))
    side = me % 2
    halves = [jnp.where(side == 0, mine, other), jnp.where(side == 0, other, mine)]
    adjoint = jnp.concatenate(halves, axis=2)
    cond = functools.reduce(jnp.add, parts)
    return (adjoint[None], cond, storage[:members, 0])


def solution(mesh):
    placed = (
        P("tm", None, "tile", None),
        P("tile", None),
        P("tile", None),
        P("tile", None),
        P(None, "tile", None),
        P("tm", None, None),
        P("tm", None, None, None),
        P(),
    )
    return jax.shard_map(
        shards,
        mesh=mesh,
        in_specs=placed,
        out_specs=(P("tm", None, "tile", None), P("tile", "tm"), P()),
        check_vma=False,
    )
```
